128 devices in a mesh: section: 4 (over y), expert: 32 (over x, z, core).
Axes of the slice: x: 4, y: 4, z: 4, core: 2. Of those that a mesh axis runs over, the one named last changes fastest.
Arguments:
- tokens: bfloat16 [4, 1024, 4096], P('section', 'expert'), may hold values from -6 to 6
- w_in: bfloat16 [2, 4, 2, 4096, 12288], P(None, 'section', None, None, 'expert'), may hold values from -0.09375 to 0.09375
- w_down: bfloat16 [2, 4, 12288, 4096], P(None, 'section', 'expert'), may hold values from -0.15625 to 0.15625
- norm_gain: float32 [2, 4, 4096], P(None, 'section'), may hold values from 0.1 to 1.9
- route_ids: int32 [2, 4, 4, 1024, 8], P(None, 'section', None, 'expert'), may hold values from 0 to 127, as said below
- gate_values: float32 [2, 4, 4, 1024, 8], P(None, 'section', None, 'expert'), may hold values from 0.4 to 1.6
Outputs:
- mixed: bfloat16 [4, 1024, 4096], P('section', 'expert')
The draws below stay inside these ranges and needn't reach their ends.
Inputs may be any that keep to these rules, and one draw needn't show every extreme that they name: `route_ids`: each row names 8 different experts; among the 32 rows of one device for one layer and micro-batch, no expert is named by more than 4 rows; in every layer and micro-batch some expert below 8 is named by exactly 4 rows of every device.
All inputs are finite; a program needn't handle non-finite values.
Results may differ from the reference program's by a relative error of at most 0.04.
Values may be sent and summed in bfloat16 or wider, within the bound.
No kernel may reach another device: no remote copies, remote signals or barrier semaphores. Data moves between devices by JAX's collectives and lax.ppermute only.
A program may use at most 64 MiB of HBM per device.

```python
import math
import jax
import jax.numpy as jnp
from jax import lax

D = 4096
FF = 1536
NROUTE = 128
TOPK = 8
SPLIT = 4
REPEATS = 2
TOK_DEV = 32
CAP = 4
SECTIONS = 4
MICRO = 4
LAYERS = 8
EXPERTS = 8
ROWS = 1024
N_EXPERT = 32


def block_routes(block_key, favored):
    key_window, key_order, key_full, key_some, key_extra, key_rows = jax.random.split(block_key, 6)
    slot_count = TOK_DEV * TOPK
    window_perm = jax.random.permutation(key_window, EXPERTS).astype(jnp.int32)
    window_perm = jnp.where(window_perm == favored, window_perm[0], window_perm)
    window_perm = window_perm.at[0].set(favored)
    window_rank = jnp.argsort(window_perm, stable=True).astype(jnp.int32)
    spread_rank = jax.random.permutation(key_order, NROUTE).astype(jnp.int32)
    full_block = jax.random.randint(key_full, (), 0, 4) != 0
    some_count = jax.random.randint(key_some, (), 1, EXPERTS + 1).astype(jnp.int32)
    window_hot = jnp.where(full_block, jnp.int32(EXPERTS), some_count)
    most_hot = max(EXPERTS, slot_count // (2 * CAP))
    extra_hot = jax.random.randint(key_extra, (), 0, most_hot - window_hot + 1).astype(jnp.int32)
    hot_count = window_hot + extra_hot
    ranking = jnp.arange(NROUTE, dtype=jnp.int32)
    rank_full = jnp.concatenate([window_rank, jnp.zeros((NROUTE - EXPERTS,), jnp.int32)])
    window_score = jnp.where(rank_full < window_hot, rank_full, 2 * NROUTE + spread_rank)
    score = jnp.where(ranking < EXPERTS, window_score, NROUTE + spread_rank).astype(jnp.int32)
    order = jnp.argsort(score, stable=True).astype(jnp.int32)
    remaining = slot_count - hot_count * CAP
    others = jnp.maximum(NROUTE - hot_count, 1)
    lower = remaining // others
    surplus = remaining - lower * others
    counts = jnp.where(ranking < hot_count, jnp.int32(CAP), lower + (ranking - hot_count < surplus).astype(jnp.int32))
    bounds = jnp.cumsum(counts).astype(jnp.int32)
    position = jnp.arange(slot_count, dtype=jnp.int32)
    owner_rank = jnp.searchsorted(bounds, position, side='right').astype(jnp.int32)
    picked = order[owner_rank].reshape(TOPK, TOK_DEV).T
    shuffle = jax.random.permutation(key_rows, TOK_DEV)
    return picked[shuffle]


def draw_route_ids(key, part):
    key = jax.random.fold_in(key, 11)
    layer_key, block_key = jax.random.split(key)
    groups = REPEATS * SECTIONS * MICRO
    block_count = ROWS // TOK_DEV
    favored = jax.random.randint(layer_key, (groups,), 0, EXPERTS).astype(jnp.int32)
    block_keys = jax.random.split(block_key, groups * block_count)
    favored_all = jnp.repeat(favored, block_count)
    routes = jax.vmap(block_routes)(block_keys, favored_all)
    return routes.reshape(REPEATS, SECTIONS, MICRO, ROWS, TOPK).astype(jnp.int32)


def shard_levels(stream_key, shape, cuts, low, largest):
    factor_of = 1.0
    for axis_at, shards_of in cuts:
        steps = jax.random.uniform(jax.random.fold_in(jax.random.fold_in(stream_key, 6), axis_at), (shards_of,), jnp.float32, low / len(cuts), largest / len(cuts))
        factor_of = factor_of * jnp.repeat(jnp.exp(steps), shape[axis_at] // shards_of).reshape((-1,) + (1,) * (len(shape) - 1 - axis_at))
    return factor_of


def bell_draw(rng, extent, width, most, shards=(), kind=jnp.bfloat16):
    values = jax.random.normal(rng, extent, jnp.float32) * width
    if len(shards) > 0:
        values = shard_levels(rng, extent, shards, -0.22, 0.18) * values
    return jnp.clip(values, min=-most, max=most).astype(kind)


def setup_inputs(seed: int = 0) -> dict:
    seeds = jax.random.split(jax.random.key(seed), 7)
    return {
        "tokens": bell_draw(seeds[0], (MICRO, ROWS, D), 1.0, 6.0, ((0, 4), (1, 32))),
        "w_in": bell_draw(seeds[1], (REPEATS, SECTIONS, 2, D, EXPERTS * FF), D ** -0.5, 0.09375, ((1, 4), (4, 32))),
        "w_down": bell_draw(seeds[2], (REPEATS, SECTIONS, EXPERTS * FF, D), FF ** -0.5, 0.15625, ((1, 4), (2, 32))),
        "norm_gain": jnp.clip(1.0 + 0.18 * jax.random.normal(seeds[3], (REPEATS, SECTIONS, D), jnp.float32), 0.1, 1.9),
        "route_ids": draw_route_ids(jax.random.fold_in(seeds[6], 71), 0),
        "gate_values": jnp.clip(jnp.exp(math.log(1.6) - 1.3862944 * jax.random.uniform(seeds[5], (REPEATS, SECTIONS, MICRO, ROWS, TOPK), jnp.float32) ** shard_levels(seeds[5], (REPEATS, SECTIONS, MICRO, ROWS, TOPK), ((1, 4), (3, 32)), -0.2, 0.2)), 0.4, 1.6),
    }


def row_slots(route_rows, gate_rows, n_window, capacity):
    window = jnp.arange(n_window, dtype=jnp.int32)
    match_table = route_rows[:, :, None] == window[None, None, :]
    chosen = jnp.any(match_table, axis=1)
    weight = lax.optimization_barrier(jnp.sum(jnp.where(match_table, gate_rows[:, :, None], jnp.float32(0.0)), axis=1))
    position = jnp.cumsum(chosen.astype(jnp.int32), axis=0) - 1
    places = jnp.arange(capacity, dtype=jnp.int32)
    onehot = jnp.logical_and(position[:, :, None] == places[None, None, :], chosen[:, :, None])
    return (onehot, weight)

def normalize(values, gain):
    scale = lax.rsqrt(lax.optimization_barrier(jnp.mean(values * values, axis=-1, keepdims=True)) + 1e-06)
    return (values * scale * gain.astype(jnp.float32)).astype(jnp.bfloat16)

def expert_rows(rows, weight_in, weight_down):
    part_width = FF // SPLIT
    total = jnp.zeros((rows.shape[0], D), jnp.float32)
    for piece in range(SPLIT):
        lower = piece * part_width
        gate = jnp.dot(rows, weight_in[0][:, lower:lower + part_width], preferred_element_type=jnp.float32)
        upward = jnp.dot(rows, weight_in[1][:, lower:lower + part_width], preferred_element_type=jnp.float32)
        hidden = (jax.nn.silu(gate) * upward).astype(jnp.bfloat16)
        partial_out = jnp.dot(hidden, weight_down[lower:lower + part_width], preferred_element_type=jnp.float32).astype(jnp.bfloat16)
        partial_out = lax.optimization_barrier(partial_out)
        total = total + partial_out.astype(jnp.float32)
    return total

def run_layer(state, repeat, section, micro, w_in, w_down, norm_gain, route_ids, gate_values):
    values = state.astype(jnp.float32)
    normed = normalize(values, norm_gain[repeat, section])
    routes = route_ids[repeat, section, micro].reshape(N_EXPERT, TOK_DEV, TOPK)
    gates = gate_values[repeat, section, micro].reshape(N_EXPERT, TOK_DEV, TOPK)
    onehot, weight = jax.vmap(row_slots, in_axes=(0, 0, None, None))(routes, gates, EXPERTS, CAP)
    blocks = normed.reshape(N_EXPERT, TOK_DEV, D)
    buffer = jnp.einsum('brec,brd->ebcd', onehot.astype(jnp.float32), blocks.astype(jnp.float32)).astype(jnp.bfloat16)
    buffer = buffer.reshape(EXPERTS, N_EXPERT * CAP, D)
    weights_in = w_in[repeat, section].reshape(2, D, EXPERTS, FF).transpose(2, 0, 1, 3)
    weights_down = w_down[repeat, section].reshape(EXPERTS, FF, D)

    def one_expert(item):
        return expert_rows(item[0], item[1], item[2])
    outputs = lax.map(one_expert, (buffer, weights_in, weights_down))
    outputs = outputs.reshape(EXPERTS, N_EXPERT, CAP, D)
    mixing = onehot.astype(jnp.float32) * weight[:, :, :, None]
    update = jnp.einsum('brec,ebcd->brd', mixing, outputs).reshape(ROWS, D)
    result = (values + update).astype(jnp.bfloat16)
    return lax.optimization_barrier(result)

def reference(tokens, w_in, w_down, norm_gain, route_ids, gate_values):
    results = []
    for micro in range(MICRO):
        state = tokens[micro]
        for layer_index in range(LAYERS):
            repeat = layer_index // SECTIONS
            section = layer_index % SECTIONS
            state = run_layer(state, repeat, section, micro, w_in, w_down, norm_gain, route_ids, gate_values)
        results.append(state)
    return jnp.stack(results)
```

```python
import functools

import jax
import jax.numpy as jnp
from jax import lax
from jax.experimental import pallas as pl
from jax.experimental.pallas import tpu as pltpu
from jax.sharding import Mesh
from jax.sharding import PartitionSpec as P

SPLIT = 4
CAP = 4
CHIPS = ("x", "z")
SWAP = [(0, 1), (1, 0)]

IN_VMEM = pl.BlockSpec(memory_space=pltpu.VMEM)
IN_SMEM = pl.BlockSpec(memory_space=pltpu.SMEM)
IN_HBM = pl.BlockSpec(memory_space=pltpu.HBM)
MIB = 2**20
EARLY = ((0,), (1,), (2, 3))


def dot(a, b):
    return jnp.dot(a, b, preferred_element_type=jnp.float32)


def dot_first(a, b):
    return lax.dot_general(a, b, (((0,), (0,)), ((), ())), preferred_element_type=jnp.float32)


def as_bf16(mask):
    return mask.astype(jnp.float32).astype(jnp.bfloat16)


def schedule(step, section, sections, layers):
    micro = lax.rem(section[0] - step + 16 * sections, sections)
    level = step - lax.rem(sections - micro, sections)
    active = jnp.logical_and(level >= 0, level < layers)
    repeat = jnp.where(level >= sections, 1, 0)
    return repeat, repeat * sections + micro, active


def table_kernel(ids, gates, hot, mix):
    groups, rows, topk = ids.shape
    wide = hot.shape[2]
    column = lax.broadcasted_iota(jnp.int32, (rows, wide), 1)
    expert = column // (2 * CAP * (SPLIT // 2))
    slot = column - column // CAP * CAP
    half = column // CAP - column // (2 * CAP) * 2
    earlier = as_bf16(lax.broadcasted_iota(jnp.int32, (rows, rows), 0) > lax.broadcasted_iota(jnp.int32, (rows, rows), 1))
    for group in range(groups):
        chosen = jnp.zeros((rows, wide), jnp.float32)
        weight = jnp.zeros((rows, wide), jnp.float32)
        for k in range(topk):
            match = ids[group, :, k : k + 1] == expert
            chosen = jnp.where(match, 1.0, chosen)
            weight = jnp.where(match, weight + gates[group, :, k : k + 1], weight)
        position = dot(earlier, chosen.astype(jnp.bfloat16))
        taken = jnp.where(position == slot.astype(jnp.float32), chosen, 0.0)
        for k in range(2):
            here = jnp.where(half == k, taken, 0.0)
            scaled = here * weight
            high = scaled.astype(jnp.bfloat16)
            hot[group, k * rows : (k + 1) * rows, :] = here.astype(jnp.bfloat16)
            mix[0, group, k * rows : (k + 1) * rows, :] = high
            mix[1, group, k * rows : (k + 1) * rows, :] = (scaled - high.astype(jnp.float32)).astype(jnp.bfloat16)


def pack_kernel(when, section, x, gain, hot, out):
    repeat, group, _ = when(section)
    values = x[...].astype(jnp.float32)
    scale = lax.rsqrt(jnp.mean(values * values, axis=-1, keepdims=True) + 1e-06)
    normed = (values * scale * gain[pl.ds(repeat, 1), :]).astype(jnp.bfloat16)
    half = normed.shape[1] // 2
    stacked = jnp.concatenate([normed[:, :half], normed[:, half:]], axis=0)
    out[...] = dot_first(hot[group], stacked).astype(jnp.bfloat16)


def place(rows, columns, offset, transposed):
    shape = (columns, rows) if transposed else (rows, columns)
    row = lax.broadcasted_iota(jnp.int32, shape, int(transposed))
    column = lax.broadcasted_iota(jnp.int32, shape, 1 - int(transposed))
    block = column // (2 * CAP)
    inner = column - block * (2 * CAP) - offset
    return as_bf16((block * CAP + inner == row) & (inner >= 0) & (inner < CAP))


def gather_rows(rows, x):
    wide, half = rows.shape
    got = rows[...]
    for k in range(2):
        x[:, k * half : (k + 1) * half] = dot(place(wide // 2, wide, k * CAP, False), got).astype(jnp.bfloat16)


def hidden_rows(x, w_in):
    given = x[...]
    count = given.shape[0]
    gate = dot(given, w_in[0])
    upward = dot(given, w_in[1])
    part = (gate / (1.0 + jnp.exp(-gate)) * upward).astype(jnp.bfloat16)
    return [dot(place(count, 2 * count, k * CAP, True), part).astype(jnp.bfloat16) for k in range(2)]


def down_rows(hidden, downs, out):
    half = out.shape[1]
    pieces = 4
    size = half // pieces
    for j in range(pieces):
        total = None
        for k in range(2):
            for spread, w_down in zip(hidden, downs):
                partial = dot(spread[k], w_down[:, k * half + j * size : k * half + (j + 1) * size])
                total = partial if total is None else total + partial
        out[:, j * size : (j + 1) * size] = total.astype(jnp.bfloat16)


def experts(rows, x, held, repeat, out):
    gather_rows(rows, x)
    hidden = [hidden_rows(x, w.at[repeat]) for w in held[:2]]
    down_rows(hidden, [w.at[repeat] for w in held[2:]], out)


def first_expert_kernel(rows, *refs):
    given, out, held, (x, sems) = refs[:4], refs[4], refs[5:9], refs[9:]
    copies = [
        pltpu.make_async_copy(source.at[0, 0], to.at[0], sems.at[k]) for k, (source, to) in enumerate(zip(given, held))
    ]
    for copy in copies:
        copy.start()
    gather_rows(rows, x)
    hidden = []
    for k in range(2):
        copies[k].wait()
        hidden.append(hidden_rows(x, held[k].at[0]))
    for copy in copies[2:]:
        copy.wait()
    down_rows(hidden, [w.at[0] for w in held[2:]], out)


def early_expert_kernel(parts, rows, *refs):
    given, refs = refs[: len(parts)], refs[len(parts) :]
    held, out, after, (x, sems) = refs[:4], refs[4], refs[5:9], refs[9:]
    copies = [
        pltpu.make_async_copy(source.at[1, 0], after[k].at[1], sems.at[n]) for n, (source, k) in enumerate(zip(given, parts))
    ]
    for copy in copies:
        copy.start()
    experts(rows, x, held, 0, out)
    for copy in copies:
        copy.wait()


def expert_kernel(when, section, rows, *refs):
    repeat, _, _ = when(section)
    experts(rows, refs[-1], refs[:4], repeat, refs[4])


def mix_kernel(when, section, x, returned, mix, out):
    _, group, active = when(section)
    got = returned[...]
    update = dot(mix[0, group], got) + dot(mix[1, group], got)
    rows = x.shape[0]
    update = jnp.concatenate([update[:rows], update[rows:]], axis=1)
    values = x[...].astype(jnp.float32)
    out[...] = jnp.where(active, values + update, values).astype(jnp.bfloat16)


def kernel(name, function, out_shape, in_specs, limit=4, scratch=(), aliases=None):
    return pl.pallas_call(
        function,
        out_shape=out_shape,
        in_specs=in_specs,
        out_specs=jax.tree.map(lambda _: IN_VMEM, out_shape),
        scratch_shapes=list(scratch),
        input_output_aliases=aliases or {},
        compiler_params=pltpu.CompilerParams(vmem_limit_bytes=limit * MIB),
        name=name,
    )


def body(tokens, w_in, w_down, norm_gain, route_ids, gate_values):
    sections = lax.axis_size("section")
    chips = lax.axis_size("x") * lax.axis_size("z")
    repeats, _, micros, rows, topk = route_ids.shape
    layers = repeats * sections
    steps = layers + sections - 1
    groups = repeats * micros
    section = lax.axis_index("section").astype(jnp.int32).reshape(1)
    width = tokens.shape[-1]
    slots = chips * 2 * CAP
    bf16 = lambda *shape: jax.ShapeDtypeStruct(shape, jnp.bfloat16)

    hot, mix = kernel(
        "tables", table_kernel, (bf16(groups, 2 * rows, slots), bf16(2, groups, 2 * rows, slots)), [IN_VMEM] * 2
    )(route_ids.reshape(groups, rows, topk), gate_values.reshape(groups, rows, topk))
    gain = norm_gain.reshape(repeats, width)

    def kept(*arrays):
        return [pltpu.with_memory_space_constraint(a, pltpu.VMEM) for a in arrays]

    def outside(*arrays):
        return [pltpu.with_memory_space_constraint(a, pltpu.HBM) for a in arrays]

    given = (w_in, lax.ppermute(w_in, "core", SWAP), w_down, lax.ppermute(w_down, "core", SWAP))
    held = tuple(pltpu.VMEM((repeats,) + w.shape[2:], jnp.bfloat16) for w in given)
    wide = bf16(slots, width // 2)

    def across(v):
        v = v.reshape(chips, 2 * CAP, width // 2)
        v = lax.all_to_all(v, CHIPS, split_axis=0, concat_axis=0, tiled=True)
        return v.reshape(slots, width // 2)

    def relay(v, by):
        return lax.ppermute(v, "section", [(i, (i + by) % sections) for i in range(sections)])

    state = tokens[0]
    for step in range(steps):
        when = functools.partial(schedule, step, sections=sections, layers=layers)
        packed = kernel("norm_pack", functools.partial(pack_kernel, when), wide, [IN_SMEM] + [IN_VMEM] * 3)(
            section, state, gain, hot
        )
        arrived = across(packed)
        x = pltpu.VMEM((slots // 2, width), jnp.bfloat16)
        if step == 0:
            outputs, *weights = kernel(
                "first_experts",
                first_expert_kernel,
                (wide, *held),
                [IN_VMEM] + [IN_HBM] * 4,
                scratch=[x, pltpu.SemaphoreType.DMA((4,))],
            )(arrived, *outside(*given))
        elif step <= len(EARLY):
            parts = EARLY[step - 1]
            outputs, *weights = kernel(
                "early_experts",
                functools.partial(early_expert_kernel, parts),
                (wide, *held),
                [IN_VMEM] + [IN_HBM] * len(parts) + [IN_VMEM] * 4,
                scratch=[x, pltpu.SemaphoreType.DMA((2,))],
                aliases={1 + len(parts) + k: 1 + k for k in range(4)},
            )(arrived, *outside(*(given[k] for k in parts)), *kept(*weights))
        else:
            outputs, *weights = kernel(
                "experts",
                functools.partial(expert_kernel, when),
                (wide, *held),
                [IN_SMEM] + [IN_VMEM] * 5,
                scratch=[x],
                aliases={2 + k: 1 + k for k in range(4)},
            )(section, arrived, *kept(*weights))
        returned = across(outputs)
        mixed = kernel("mix", functools.partial(mix_kernel, when), bf16(rows, width), [IN_SMEM] + [IN_VMEM] * 3)(
            section, state, returned, mix
        )
        if step < steps - 1:
            state = relay(mixed, 1)
    waiting = relay(state, 2)
    last = lax.ppermute(mixed, "section", [(sections - 1, 1)])
    return jnp.where(section[0] == 1, last, waiting)[None]


def solution(mesh):
    fine = Mesh(mesh.devices.reshape(4, 4, 4, 2), ("section", "x", "z", "core"))
    expert = ("x", "z", "core")
    return jax.shard_map(
        body,
        mesh=fine,
        in_specs=(
            P("section", expert, None),
            P(None, "section", None, None, expert),
            P(None, "section", expert, None),
            P(None, "section", None),
            P(None, "section", None, expert, None),
            P(None, "section", None, expert, None),
        ),
        out_specs=P("section", expert, None),
        check_vma=False,
    )
```

```python
import functools

import jax
import jax.numpy as jnp
from jax import lax
from jax.experimental import pallas as pl
from jax.experimental.pallas import tpu as pltpu
from jax.sharding import Mesh
from jax.sharding import PartitionSpec as P

SPLIT = 4
CAP = 4
CHIPS = ("x", "z")
SWAP = [(0, 1), (1, 0)]

IN_VMEM = pl.BlockSpec(memory_space=pltpu.VMEM)
IN_SMEM = pl.BlockSpec(memory_space=pltpu.SMEM)
IN_HBM = pl.BlockSpec(memory_space=pltpu.HBM)
MIB = 2**20


def dot(a, b):
    return jnp.dot(a, b, preferred_element_type=jnp.float32)


def dot_first(a, b):
    return lax.dot_general(a, b, (((0,), (0,)), ((), ())), preferred_element_type=jnp.float32)


def as_bf16(mask):
    return mask.astype(jnp.float32).astype(jnp.bfloat16)


def schedule(step, section, sections, layers):
    behind = step - section[0]
    micro = lax.rem(behind + sections, sections)
    repeat = jnp.where(behind >= sections, 1, 0)
    active = jnp.logical_and(behind >= 0, behind < layers)
    return repeat, repeat * sections + micro, active


def relay_pairs(step, sections, layers):
    if step == 0:
        return [(k, k ^ 1) for k in range(sections)]
    home = step - layers + 1
    if home < 1:
        return [(k, (k + 1) % sections) for k in range(sections)]
    return [(k, k) for k in range(home)] + [(k, k + 1) for k in range(home, sections - 1)] + [(sections - 1, home)]


def make_tables(ids, gates, hot, mix):
    repeats, _, micros, topk, rows = ids.shape
    wide = hot.shape[1]
    place = lax.broadcasted_iota(jnp.int32, (wide, rows), 0)
    expert = place // (2 * CAP * (SPLIT // 2))
    slot = place - place // CAP * CAP
    half = place // CAP - place // (2 * CAP) * 2
    earlier = as_bf16(lax.broadcasted_iota(jnp.int32, (rows, rows), 0) < lax.broadcasted_iota(jnp.int32, (rows, rows), 1))
    for group in range(repeats * micros):
        named = ids[group // micros, 0, group % micros]
        given = gates[group // micros, 0, group % micros]
        chosen = jnp.zeros((wide, rows), jnp.float32)
        weight = jnp.zeros((wide, rows), jnp.float32)
        for k in range(topk):
            match = named[k : k + 1, :] == expert
            chosen = jnp.where(match, 1.0, chosen)
            weight = jnp.where(match, weight + given[k : k + 1, :], weight)
        position = dot(chosen.astype(jnp.bfloat16), earlier)
        taken = jnp.where(position == slot.astype(jnp.float32), chosen, 0.0)
        here = jnp.concatenate([jnp.where(half == k, taken, 0.0) for k in range(2)], axis=1)
        scaled = here * jnp.concatenate([weight, weight], axis=1)
        high = scaled.astype(jnp.bfloat16)
        hot[group] = here.astype(jnp.bfloat16)
        mix[0, group] = high
        mix[1, group] = (scaled - high.astype(jnp.float32)).astype(jnp.bfloat16)


def pack_kernel(when, section, x, gain, hot, out):
    repeat, group, _ = when(section)
    values = x[...].astype(jnp.float32)
    scale = lax.rsqrt(jnp.mean(values * values, axis=-1, keepdims=True) + 1e-06)
    normed = (values * scale * gain[repeat]).astype(jnp.bfloat16)
    half = normed.shape[1] // 2
    stacked = jnp.concatenate([normed[:, :half], normed[:, half:]], axis=0)
    out[...] = dot(hot[group], stacked).astype(jnp.bfloat16)


def first_pack_kernel(when, section, x, gain, ids, gates, out, hot, mix):
    make_tables(ids, gates, hot, mix)
    pack_kernel(when, section, x, gain, hot, out)


def place(rows, columns, offset, transposed):
    shape = (columns, rows) if transposed else (rows, columns)
    row = lax.broadcasted_iota(jnp.int32, shape, int(transposed))
    column = lax.broadcasted_iota(jnp.int32, shape, 1 - int(transposed))
    block = column // (2 * CAP)
    inner = column - block * (2 * CAP) - offset
    return as_bf16((block * CAP + inner == row) & (inner >= 0) & (inner < CAP))


def gather_rows(rows, x, start=0):
    wide, half = rows.shape
    got = rows[...]
    for k in range(2):
        x[start : start + wide // 2, k * half : (k + 1) * half] = dot(place(wide // 2, wide, k * CAP, False), got).astype(jnp.bfloat16)


def gated(gate, upward):
    return (gate / (1.0 + jnp.exp(-gate)) * upward).astype(jnp.bfloat16)


def dot_halves(x, held, repeat, columns):
    half = x.shape[1] // 2
    return dot(x[:, :half], held[0][repeat, :, columns]) + dot(x[:, half:], held[1][repeat, :, columns])


def core_hidden(x, held, repeat, who):
    size = held[0].shape[2] // 4
    return gated(*(dot_halves(x, held, repeat, slice((2 * g + who) * size, (2 * g + who + 1) * size)) for g in range(2)))


def down_rows(hidden, downs, out):
    count = hidden.shape[0]
    spread = [dot(place(count, 2 * count, k * CAP, True), hidden).astype(jnp.bfloat16) for k in range(2)]
    pieces = 4
    size = out.shape[1] // pieces
    for j in range(pieces):
        columns = slice(j * size, (j + 1) * size)
        total = dot(spread[0], downs[0][:, columns]) + dot(spread[1], downs[1][:, columns])
        out[:, columns] = total.astype(out.dtype)


def weight_copies(w_in, w_down, repeat, who, held, sems):
    half = held[0].shape[1]
    size = w_in.shape[4]
    pairs = []
    for k in range(2):
        part = pl.ds(k * half, half)
        for g in range(2):
            pairs.append((w_in.at[repeat, 0, g, part, :], held[k].at[repeat, :, pl.ds((2 * g + who) * size, size)]))
    for k in range(2):
        part = pl.ds(k * half, half)
        pairs.append((w_down.at[repeat, 0, :, part], held[2 + k].at[repeat, pl.ds(who * size, size), :]))
    copies = [pltpu.make_async_copy(source, to, sems.at[n]) for n, (source, to) in enumerate(pairs)]
    for copy in copies:
        copy.start()
    return copies


def first_expert_kernel(rows, rows_other, w_in, w_down, out, out_other, *refs):
    held, (x, sems) = refs[:4], refs[4:]
    copies = weight_copies(w_in, w_down, 0, 0, held, sems)
    count = rows.shape[0] // 2
    gather_rows(rows, x)
    gather_rows(rows_other, x, count)
    for copy in copies[:4]:
        copy.wait()
    hidden = core_hidden(x, held, 0, 0)
    for copy in copies[4:]:
        copy.wait()
    size = hidden.shape[1]
    downs = [w.at[0, :size] for w in held[2:]]
    down_rows(hidden[count:], downs, out_other)
    down_rows(hidden[:count], downs, out)


def add_kernel(a, b, out):
    out[...] = (a[...] + b[...].astype(jnp.float32)).astype(jnp.bfloat16)


def experts(rows, x, held, repeat, out):
    gather_rows(rows, x)
    both = dot_halves(x, held, repeat, slice(None))
    size = both.shape[1] // 2
    down_rows(gated(both[:, :size], both[:, size:]), [w.at[repeat] for w in held[2:]], out)


def second_expert_kernel(rows, w_in, w_down, *refs):
    held, out, after, (x, sems) = refs[:4], refs[4], refs[5:9], refs[9:]
    copies = weight_copies(w_in, w_down, 0, 1, after, sems)
    gather_rows(rows, x)
    hidden = [core_hidden(x, held, 0, 0)]
    for copy in copies[:4]:
        copy.wait()
    hidden.append(core_hidden(x, after, 0, 1))
    for copy in copies[4:]:
        copy.wait()
    down_rows(jnp.concatenate(hidden, axis=1), [w.at[0] for w in after[2:]], out)


def early_expert_kernel(who, rows, w_in, w_down, *refs):
    held, out, after, (x, sems) = refs[:4], refs[4], refs[5:9], refs[9:]
    copies = weight_copies(w_in, w_down, 1, who, after, sems)
    experts(rows, x, held, 0, out)
    for copy in copies:
        copy.wait()


def expert_kernel(when, section, rows, *refs):
    repeat, _, _ = when(section)
    experts(rows, refs[-1], refs[:4], repeat, refs[4])


def mix_kernel(when, section, x, returned, mix, out):
    _, group, active = when(section)
    got = returned[...]
    update = dot_first(mix[0, group], got) + dot_first(mix[1, group], got)
    rows = x.shape[0]
    update = jnp.concatenate([update[:rows], update[rows:]], axis=1)
    values = x[...].astype(jnp.float32)
    out[...] = jnp.where(active, values + update, values).astype(jnp.bfloat16)


def kernel(name, function, out_shape, in_specs, limit=4, scratch=(), aliases=None):
    return pl.pallas_call(
        function,
        out_shape=out_shape,
        in_specs=in_specs,
        out_specs=jax.tree.map(lambda _: IN_VMEM, out_shape),
        scratch_shapes=list(scratch),
        input_output_aliases=aliases or {},
        compiler_params=pltpu.CompilerParams(vmem_limit_bytes=limit * MIB),
        name=name,
    )


def body(tokens, w_in, w_down, norm_gain, route_ids, gate_values):
    sections = lax.axis_size("section")
    chips = lax.axis_size("x") * lax.axis_size("z")
    repeats, _, micros, rows, _ = route_ids.shape
    layers = repeats * sections
    steps = layers + sections - 1
    groups = repeats * micros
    section = lax.axis_index("section").astype(jnp.int32).reshape(1)
    width = tokens.shape[-1]
    slots = chips * 2 * CAP
    bf16 = lambda *shape: jax.ShapeDtypeStruct(shape, jnp.bfloat16)

    def kept(*arrays):
        return [pltpu.with_memory_space_constraint(a, pltpu.VMEM) for a in arrays]

    def outside(*arrays):
        return [pltpu.with_memory_space_constraint(a, pltpu.HBM) for a in arrays]

    hidden = w_in.shape[-1]
    held = (pltpu.VMEM((repeats, width // 2, 4 * hidden), jnp.bfloat16),) * 2 + (
        pltpu.VMEM((repeats, 2 * hidden, width // 2), jnp.bfloat16),
    ) * 2
    wide = bf16(slots, width // 2)
    dma = pltpu.SemaphoreType.DMA((6,))

    def across(v):
        v = v.reshape(chips, 2 * CAP, width // 2)
        v = lax.all_to_all(v, CHIPS, split_axis=0, concat_axis=0, tiled=True)
        return v.reshape(slots, width // 2)

    def other_core(v):
        return lax.ppermute(v, "core", SWAP)

    state = tokens[0]
    for step in range(steps):
        when = functools.partial(schedule, step, sections=sections, layers=layers)
        if step == 0:
            packed, hot, mix = kernel(
                "first_norm_pack",
                functools.partial(first_pack_kernel, when),
                (wide, bf16(groups, slots, 2 * rows), bf16(2, groups, slots, 2 * rows)),
                [IN_SMEM] + [IN_VMEM] * 4,
            )(section, *outside(state, norm_gain, jnp.swapaxes(route_ids, 3, 4), jnp.swapaxes(gate_values, 3, 4)))
        else:
            packed = kernel("norm_pack", functools.partial(pack_kernel, when), wide, [IN_SMEM] + [IN_VMEM] * 3)(
                section, state, norm_gain, hot
            )
        arrived = across(packed)
        x = pltpu.VMEM((slots // 2, width), jnp.bfloat16)
        if step == 0:
            own, outputs, *weights = kernel(
                "first_experts",
                first_expert_kernel,
                (jax.ShapeDtypeStruct(wide.shape, jnp.float32), wide, *held),
                [IN_VMEM] * 2 + [IN_HBM] * 2,
                scratch=[pltpu.VMEM((slots, width), jnp.bfloat16), dma],
                limit=6,
            )(arrived, other_core(arrived), *outside(w_in, w_down))
            outputs = kernel("add", add_kernel, wide, [IN_VMEM] * 2)(own, other_core(outputs))
            late_in, late_down, outputs = lax.optimization_barrier((w_in, w_down, outputs))
            sources = ((w_in, w_down), (other_core(late_in), other_core(late_down)))
        elif step == 1:
            outputs, *weights = kernel(
                "second_experts",
                second_expert_kernel,
                (wide, *held),
                [IN_VMEM] + [IN_HBM] * 2 + [IN_VMEM] * 4,
                scratch=[x, dma],
                aliases={3 + k: 1 + k for k in range(4)},
            )(arrived, *outside(*sources[1]), *kept(*weights))
        elif step < 4:
            outputs, *weights = kernel(
                "early_experts",
                functools.partial(early_expert_kernel, step - 2),
                (wide, *held),
                [IN_VMEM] + [IN_HBM] * 2 + [IN_VMEM] * 4,
                scratch=[x, dma],
                aliases={3 + k: 1 + k for k in range(4)},
            )(arrived, *outside(*sources[step - 2]), *kept(*weights))
        else:
            outputs, *weights = kernel(
                "experts",
                functools.partial(expert_kernel, when),
                (wide, *held),
                [IN_SMEM] + [IN_VMEM] * 5,
                scratch=[x],
                aliases={2 + k: 1 + k for k in range(4)},
            )(section, arrived, *kept(*weights))
        returned = across(outputs)
        state = kernel("mix", functools.partial(mix_kernel, when), bf16(rows, width), [IN_SMEM] + [IN_VMEM] * 3)(
            section, state, returned, mix
        )
        if step < steps - 1:
            state = lax.ppermute(state, "section", relay_pairs(step, sections, layers))
    return state[None]


def solution(mesh):
    fine = Mesh(mesh.devices.reshape(4, 4, 4, 2), ("section", "x", "z", "core"))
    expert = ("x", "z", "core")
    return jax.shard_map(
        body,
        mesh=fine,
        in_specs=(
            P("section", expert, None),
            P(None, "section", None, None, expert),
            P(None, "section", expert, None),
            P(None, "section", None),
            P(None, "section", None, expert, None),
            P(None, "section", None, expert, None),
        ),
        out_specs=P("section", expert, None),
        check_vma=False,
    )
```

```python
import functools

import jax
import jax.numpy as jnp
from jax import lax
from jax.experimental import pallas as pl
from jax.experimental.pallas import tpu as pltpu
from jax.sharding import Mesh
from jax.sharding import PartitionSpec as P

SPLIT = 4
CAP = 4
CHIPS = ("x", "z")
SWAP = [(0, 1), (1, 0)]

IN_VMEM = pl.BlockSpec(memory_space=pltpu.VMEM)
IN_SMEM = pl.BlockSpec(memory_space=pltpu.SMEM)
IN_HBM = pl.BlockSpec(memory_space=pltpu.HBM)
MIB = 2**20


def dot(a, b):
    return jnp.dot(a, b, preferred_element_type=jnp.float32)


def dot_first(a, b):
    return lax.dot_general(a, b, (((0,), (0,)), ((), ())), preferred_element_type=jnp.float32)


def as_bf16(mask):
    return mask.astype(jnp.float32).astype(jnp.bfloat16)


def schedule(step, section, sections, layers):
    behind = step - section[0]
    micro = lax.rem(behind + sections, sections)
    repeat = jnp.where(behind >= sections, 1, 0)
    active = jnp.logical_and(behind >= 0, behind < layers)
    return repeat, repeat * sections + micro, active


def relay_pairs(step, sections, layers):
    if step == 0:
        return [(k, k ^ 1) for k in range(sections)]
    home = step - layers + 1
    if home < 1:
        return [(k, (k + 1) % sections) for k in range(sections)]
    return [(k, k) for k in range(home)] + [(k, k + 1) for k in range(home, sections - 1)] + [(sections - 1, home)]


def make_tables(ids, gates, hot, mix):
    repeats, _, micros, topk, rows = ids.shape
    wide = hot.shape[1]
    place = lax.broadcasted_iota(jnp.int32, (wide, rows), 0)
    expert = place // (2 * CAP * (SPLIT // 2))
    slot = place - place // CAP * CAP
    half = place // CAP - place // (2 * CAP) * 2
    earlier = as_bf16(lax.broadcasted_iota(jnp.int32, (rows, rows), 0) < lax.broadcasted_iota(jnp.int32, (rows, rows), 1))
    for group in range(repeats * micros):
        named = ids[group // micros, 0, group % micros]
        given = gates[group // micros, 0, group % micros]
        chosen = jnp.zeros((wide, rows), jnp.float32)
        weight = jnp.zeros((wide, rows), jnp.float32)
        for k in range(topk):
            match = named[k : k + 1, :] == expert
            chosen = jnp.where(match, 1.0, chosen)
            weight = jnp.where(match, weight + given[k : k + 1, :], weight)
        position = dot(chosen.astype(jnp.bfloat16), earlier)
        taken = jnp.where(position == slot.astype(jnp.float32), chosen, 0.0)
        here = jnp.concatenate([jnp.where(half == k, taken, 0.0) for k in range(2)], axis=1)
        scaled = here * jnp.concatenate([weight, weight], axis=1)
        high = scaled.astype(jnp.bfloat16)
        hot[group] = here.astype(jnp.bfloat16)
        mix[0, group] = high
        mix[1, group] = (scaled - high.astype(jnp.float32)).astype(jnp.bfloat16)


def pack_kernel(when, section, x, gain, hot, out):
    repeat, group, _ = when(section)
    values = x[...].astype(jnp.float32)
    scale = lax.rsqrt(jnp.mean(values * values, axis=-1, keepdims=True) + 1e-06)
    normed = (values * scale * gain[repeat]).astype(jnp.bfloat16)
    half = normed.shape[1] // 2
    stacked = jnp.concatenate([normed[:, :half], normed[:, half:]], axis=0)
    out[...] = dot(hot[group], stacked).astype(jnp.bfloat16)


def first_pack_kernel(when, section, x, gain, ids, gates, out, hot, mix):
    make_tables(ids, gates, hot, mix)
    pack_kernel(when, section, x, gain, hot, out)


def place(rows, columns, offset, transposed):
    shape = (columns, rows) if transposed else (rows, columns)
    row = lax.broadcasted_iota(jnp.int32, shape, int(transposed))
    column = lax.broadcasted_iota(jnp.int32, shape, 1 - int(transposed))
    block = column // (2 * CAP)
    inner = column - block * (2 * CAP) - offset
    return as_bf16((block * CAP + inner == row) & (inner >= 0) & (inner < CAP))


def gather_rows(rows, x, start=0):
    wide, half = rows.shape
    got = rows[...]
    for k in range(2):
        x[start : start + wide // 2, k * half : (k + 1) * half] = dot(place(wide // 2, wide, k * CAP, False), got).astype(jnp.bfloat16)


def gated(gate, upward):
    return (gate / (1.0 + jnp.exp(-gate)) * upward).astype(jnp.bfloat16)


def dot_halves(x, held, repeat, columns):
    half = x.shape[1] // 2
    return dot(x[:, :half], held[0][repeat, :, columns]) + dot(x[:, half:], held[1][repeat, :, columns])


def core_hidden(x, held, repeat, who):
    size = held[0].shape[2] // 4
    return gated(*(dot_halves(x, held, repeat, slice((2 * g + who) * size, (2 * g + who + 1) * size)) for g in range(2)))


def arriving_hidden(x, held, repeat, who, copies):
    size = held[0].shape[2] // 4
    half = x.shape[1] // 2
    sums = [None, None]
    for k in range(2):
        for copy in copies[2 * k : 2 * k + 2]:
            copy.wait()
        given = x[:, k * half : (k + 1) * half]
        for g in range(2):
            found = dot(given, held[k][repeat, :, (2 * g + who) * size : (2 * g + who + 1) * size])
            sums[g] = found if k == 0 else sums[g] + found
    return gated(*sums)


def down_rows(hidden, downs, out):
    count = hidden.shape[0]
    spread = [dot(place(count, 2 * count, k * CAP, True), hidden).astype(jnp.bfloat16) for k in range(2)]
    pieces = 4
    size = out.shape[1] // pieces
    for j in range(pieces):
        columns = slice(j * size, (j + 1) * size)
        total = dot(spread[0], downs[0][:, columns]) + dot(spread[1], downs[1][:, columns])
        out[:, columns] = total.astype(out.dtype)


def weight_copies(w_in, w_down, repeat, who, held, sems):
    half = held[0].shape[1]
    size = w_in.shape[4]
    pairs = []
    for k in range(2):
        part = pl.ds(k * half, half)
        for g in range(2):
            pairs.append((w_in.at[repeat, 0, g, part, :], held[k].at[repeat, :, pl.ds((2 * g + who) * size, size)]))
    for k in range(2):
        part = pl.ds(k * half, half)
        pairs.append((w_down.at[repeat, 0, :, part], held[2 + k].at[repeat, pl.ds(who * size, size), :]))
    copies = [pltpu.make_async_copy(source, to, sems.at[n]) for n, (source, to) in enumerate(pairs)]
    for copy in copies:
        copy.start()
    return copies


def first_expert_kernel(rows, rows_other, w_in, w_down, out, out_other, *refs):
    held, (x, sems) = refs[:4], refs[4:]
    copies = weight_copies(w_in, w_down, 0, 0, held, sems)
    count = rows.shape[0] // 2
    gather_rows(rows, x)
    gather_rows(rows_other, x, count)
    hidden = arriving_hidden(x, held, 0, 0, copies)
    for copy in copies[4:]:
        copy.wait()
    size = hidden.shape[1]
    downs = [w.at[0, :size] for w in held[2:]]
    down_rows(hidden[count:], downs, out_other)
    down_rows(hidden[:count], downs, out)


def add_kernel(a, b, out):
    out[...] = (a[...] + b[...].astype(jnp.float32)).astype(jnp.bfloat16)


def experts(rows, x, held, repeat, out):
    gather_rows(rows, x)
    both = dot_halves(x, held, repeat, slice(None))
    size = both.shape[1] // 2
    down_rows(gated(both[:, :size], both[:, size:]), [w.at[repeat] for w in held[2:]], out)


def second_expert_kernel(rows, w_in, w_down, *refs):
    held, out, after, (x, sems) = refs[:4], refs[4], refs[5:9], refs[9:]
    copies = weight_copies(w_in, w_down, 0, 1, after, sems)
    gather_rows(rows, x)
    hidden = [core_hidden(x, held, 0, 0)]
    for copy in copies[:4]:
        copy.wait()
    hidden.append(core_hidden(x, after, 0, 1))
    for copy in copies[4:]:
        copy.wait()
    down_rows(jnp.concatenate(hidden, axis=1), [w.at[0] for w in after[2:]], out)


def early_expert_kernel(who, rows, w_in, w_down, *refs):
    held, out, after, (x, sems) = refs[:4], refs[4], refs[5:9], refs[9:]
    copies = weight_copies(w_in, w_down, 1, who, after, sems)
    experts(rows, x, held, 0, out)
    for copy in copies:
        copy.wait()


def expert_kernel(when, section, rows, *refs):
    repeat, _, _ = when(section)
    experts(rows, refs[-1], refs[:4], repeat, refs[4])


def mix_kernel(when, section, x, returned, mix, out):
    _, group, active = when(section)
    got = returned[...]
    update = dot_first(mix[0, group], got) + dot_first(mix[1, group], got)
    rows = x.shape[0]
    update = jnp.concatenate([update[:rows], update[rows:]], axis=1)
    values = x[...].astype(jnp.float32)
    out[...] = jnp.where(active, values + update, values).astype(jnp.bfloat16)


def kernel(name, function, out_shape, in_specs, limit=4, scratch=(), aliases=None):
    return pl.pallas_call(
        function,
        out_shape=out_shape,
        in_specs=in_specs,
        out_specs=jax.tree.map(lambda _: IN_VMEM, out_shape),
        scratch_shapes=list(scratch),
        input_output_aliases=aliases or {},
        compiler_params=pltpu.CompilerParams(vmem_limit_bytes=limit * MIB),
        name=name,
    )


def body(tokens, w_in, w_down, norm_gain, route_ids, gate_values):
    sections = lax.axis_size("section")
    chips = lax.axis_size("x") * lax.axis_size("z")
    repeats, _, micros, rows, _ = route_ids.shape
    layers = repeats * sections
    steps = layers + sections - 1
    groups = repeats * micros
    section = lax.axis_index("section").astype(jnp.int32).reshape(1)
    width = tokens.shape[-1]
    slots = chips * 2 * CAP
    bf16 = lambda *shape: jax.ShapeDtypeStruct(shape, jnp.bfloat16)

    def kept(*arrays):
        return [pltpu.with_memory_space_constraint(a, pltpu.VMEM) for a in arrays]

    def outside(*arrays):
        return [pltpu.with_memory_space_constraint(a, pltpu.HBM) for a in arrays]

    hidden = w_in.shape[-1]
    held = (pltpu.VMEM((repeats, width // 2, 4 * hidden), jnp.bfloat16),) * 2 + (
        pltpu.VMEM((repeats, 2 * hidden, width // 2), jnp.bfloat16),
    ) * 2
    wide = bf16(slots, width // 2)
    dma = pltpu.SemaphoreType.DMA((6,))

    def across(v):
        v = v.reshape(chips, 2 * CAP, width // 2)
        v = lax.all_to_all(v, CHIPS, split_axis=0, concat_axis=0, tiled=True)
        return v.reshape(slots, width // 2)

    def other_core(v):
        return lax.ppermute(v, "core", SWAP)

    state = tokens[0]
    for step in range(steps):
        when = functools.partial(schedule, step, sections=sections, layers=layers)
        if step == 0:
            packed, hot, mix = kernel(
                "first_norm_pack",
                functools.partial(first_pack_kernel, when),
                (wide, bf16(groups, slots, 2 * rows), bf16(2, groups, slots, 2 * rows)),
                [IN_SMEM] + [IN_VMEM] * 4,
            )(section, *outside(state, norm_gain, jnp.swapaxes(route_ids, 3, 4), jnp.swapaxes(gate_values, 3, 4)))
        else:
            packed = kernel("norm_pack", functools.partial(pack_kernel, when), wide, [IN_SMEM] + [IN_VMEM] * 3)(
                section, state, norm_gain, hot
            )
        arrived = across(packed)
        x = pltpu.VMEM((slots // 2, width), jnp.bfloat16)
        if step == 0:
            own, outputs, *weights = kernel(
                "first_experts",
                first_expert_kernel,
                (jax.ShapeDtypeStruct(wide.shape, jnp.float32), wide, *held),
                [IN_VMEM] * 2 + [IN_HBM] * 2,
                scratch=[pltpu.VMEM((slots, width), jnp.bfloat16), dma],
                limit=6,
            )(arrived, other_core(arrived), *outside(w_in, w_down))
            outputs = kernel("add", add_kernel, wide, [IN_VMEM] * 2)(own, other_core(outputs))
            late_in, late_down, outputs = lax.optimization_barrier((w_in, w_down, outputs))
            sources = ((w_in, w_down), (other_core(late_in), other_core(late_down)))
        elif step == 1:
            outputs, *weights = kernel(
                "second_experts",
                second_expert_kernel,
                (wide, *held),
                [IN_VMEM] + [IN_HBM] * 2 + [IN_VMEM] * 4,
                scratch=[x, dma],
                aliases={3 + k: 1 + k for k in range(4)},
            )(arrived, *outside(*sources[1]), *kept(*weights))
        elif step < 4:
            outputs, *weights = kernel(
                "early_experts",
                functools.partial(early_expert_kernel, step - 2),
                (wide, *held),
                [IN_VMEM] + [IN_HBM] * 2 + [IN_VMEM] * 4,
                scratch=[x, dma],
                aliases={3 + k: 1 + k for k in range(4)},
            )(arrived, *outside(*sources[step - 2]), *kept(*weights))
        else:
            outputs, *weights = kernel(
                "experts",
                functools.partial(expert_kernel, when),
                (wide, *held),
                [IN_SMEM] + [IN_VMEM] * 5,
                scratch=[x],
                aliases={2 + k: 1 + k for k in range(4)},
            )(section, arrived, *kept(*weights))
        returned = across(outputs)
        state = kernel("mix", functools.partial(mix_kernel, when), bf16(rows, width), [IN_SMEM] + [IN_VMEM] * 3)(
            section, state, returned, mix
        )
        if step < steps - 1:
            state = lax.ppermute(state, "section", relay_pairs(step, sections, layers))
    return state[None]


def solution(mesh):
    fine = Mesh(mesh.devices.reshape(4, 4, 4, 2), ("section", "x", "z", "core"))
    expert = ("x", "z", "core")
    return jax.shard_map(
        body,
        mesh=fine,
        in_specs=(
            P("section", expert, None),
            P(None, "section", None, None, expert),
            P(None, "section", expert, None),
            P(None, "section", None),
            P(None, "section", None, expert, None),
            P(None, "section", None, expert, None),
        ),
        out_specs=P("section", expert, None),
        check_vma=False,
    )
```
